32 devices in a mesh: tok: 16 (over z, x, core), head: 2 (over y).
Axes of the slice: x: 2, y: 2, z: 4, core: 2. Of those that a mesh axis runs over, the one named last changes fastest.
Arguments:
- qkv: bfloat16 [3, 4096, 768], P(None, 'tok', 'head'), may hold values from -8 to 8
- token_rank: int32 [12, 4096], P('head', 'tok'), may hold values from 0 to 4095, as said below
- cluster_sizes: int32 [12, 64], P('head'), may hold values from 1 to 477, as said below
- cluster_owner: int32 [12, 64], P('head'), may hold values from 0 to 15, as said below
- cache_zero: bfloat16 [4096, 768], P('tok', 'head'), may hold values from -1.796875 to 1.796875
- cache_one: bfloat16 [4096, 768], P('tok', 'head'), may hold values from -1.796875 to 1.796875
- cache_two: bfloat16 [4096, 768], P('tok', 'head'), may hold values from -1.796875 to 1.796875
- cache_uncond: bfloat16 [4096, 768], P('tok', 'head'), may hold values from -4 to 4
- norm_gain: float32 [768], replicated, may hold values from 0.5 to 1.5
- norm_bias: float32 [768], replicated, may hold values from -3 to 3
Outputs:
- normed: bfloat16 [4096, 768], P(('tok', 'head'))
- taylor_zero: bfloat16 [4096, 768], P('tok', 'head')
- taylor_one: bfloat16 [4096, 768], P('tok', 'head')
- taylor_two: bfloat16 [4096, 768], P('tok', 'head')
- taylor_three: bfloat16 [4096, 768], P('tok', 'head')
The draws below stay inside these ranges and needn't reach their ends.
Inputs may be any that keep to these rules, and one draw needn't show every extreme that they name: `token_rank`: for each head a permutation of the tokens: the position of each token when the tokens are ordered by cluster, clusters in increasing number. `cluster_sizes`: for each head the sizes sum to 4096; every head has a cluster of exactly 477 tokens. `cluster_owner`: each group holds 4 clusters of every head and at most 480 tokens of a head, a bound that some group of every head reaches; of the tokens that one index of tok holds, at most 32 of one head lie in one group, a bound reached in every draw; heads 2j and 2j + 1 together have exactly 32 of those tokens in each group.
All inputs are finite; a program needn't handle non-finite values.
Results may differ from the reference program's by a relative error of at most 0.0059.
Values may be sent and summed in bfloat16 or wider, within the bound.
A program may use at most 64 MiB of HBM per device.

```python
import math
import jax
import jax.numpy as jnp
from jax import lax

HEAD_DIM = 64
HEADS = 12
WIDTH = 768
TOK_DEV = 256
TOKENS = 4096
CLD = 4
NCLUST = 64
CAP = 480
STEP_GAP = 2
N_TOK = 16


def layout_head(operands):
    head_key, pair_key, mirror = operands
    subkeys = jax.random.split(head_key, 7)
    pair_subkeys = jax.random.split(pair_key, 3)
    sign = 1 - 2 * mirror
    pair_mean = TOK_DEV // N_TOK
    shuffle = jax.random.permutation(pair_subkeys[0], N_TOK)
    shifts = jax.random.randint(pair_subkeys[1], (N_TOK // 2,), 0, pair_mean - 1)
    shifts = shifts.at[0].set(pair_mean - 2)
    per_source = jnp.zeros((N_TOK,), jnp.int32)
    per_source = per_source.at[shuffle[0::2]].set(pair_mean + sign * shifts)
    per_source = per_source.at[shuffle[1::2]].set(pair_mean - sign * shifts)
    pattern = jax.random.permutation(pair_subkeys[2], N_TOK)
    offsets = (sign * jnp.where(pattern < N_TOK // 2, 2, -2)).astype(jnp.int32)
    sources = jnp.arange(N_TOK, dtype=jnp.int32)
    counts = per_source[None, :] + offsets[(sources[:, None] - sources[None, :]) % N_TOK]
    count_ends = jnp.cumsum(counts, axis=1)
    local_keys = jax.random.split(subkeys[3], N_TOK)
    local_place = jax.vmap(lambda one_key: jax.random.permutation(one_key, TOK_DEV))(local_keys)
    targets = jnp.sum((count_ends[:, None, :] <= local_place[:, :, None]).astype(jnp.int32), axis=2).reshape(TOKENS)
    tie_break = jax.random.permutation(subkeys[4], TOKENS)
    ordering = jnp.argsort(targets * TOKENS + tie_break, stable=True)
    global_place = jnp.zeros((TOKENS,), jnp.int32).at[ordering].set(jnp.arange(TOKENS, dtype=jnp.int32))
    group_loads = N_TOK * per_source
    load_starts = jnp.cumsum(group_loads) - group_loads
    in_group = global_place - load_starts[targets]
    cut_points = jnp.sort(jax.random.randint(subkeys[5], (N_TOK, CLD - 1), 0, (group_loads - CLD + 1)[:, None]), axis=1)
    big_group = jnp.where(mirror == 1, shuffle[1], shuffle[0])
    cut_points = cut_points.at[big_group].set(0)
    cut_edges = jnp.concatenate([jnp.zeros((N_TOK, 1), jnp.int32), cut_points, (group_loads - CLD)[:, None]], axis=1)
    split_sizes = 1 + cut_edges[:, 1:] - cut_edges[:, :-1]
    cluster_ids = jnp.sort(jax.random.permutation(subkeys[6], NCLUST).reshape(N_TOK, CLD), axis=1)
    owner_row = jnp.zeros((NCLUST,), jnp.int32).at[cluster_ids.reshape(-1)].set(jnp.repeat(jnp.arange(N_TOK, dtype=jnp.int32), CLD))
    size_row = jnp.zeros((NCLUST,), jnp.int32).at[cluster_ids.reshape(-1)].set(split_sizes.reshape(-1))
    rank_starts = jnp.cumsum(size_row) - size_row
    split_ends = jnp.cumsum(split_sizes, axis=1)
    token_ends = split_ends[targets]
    within = jnp.sum((token_ends <= in_group[:, None]).astype(jnp.int32), axis=1)
    split_starts = split_ends - split_sizes
    offset_in = in_group - split_starts[targets, within]
    cluster_of = cluster_ids[targets, within]
    rank_row = rank_starts[cluster_of] + offset_in
    return (rank_row.astype(jnp.int32), size_row.astype(jnp.int32), owner_row.astype(jnp.int32))


def shared_layout(base_key):
    head_keys = jax.random.split(jax.random.fold_in(base_key, 17), HEADS)
    pair_keys = jnp.repeat(jax.random.split(jax.random.fold_in(base_key, 23), HEADS // 2), 2, axis=0)
    mirror = (jnp.arange(HEADS, dtype=jnp.int32) % 2).astype(jnp.int32)
    return lax.map(layout_head, (head_keys, pair_keys, mirror))


def draw_token_rank(key, part):
    return shared_layout(key)[0]


def draw_cluster_sizes(key, part):
    return shared_layout(key)[1]


def draw_cluster_owner(key, part):
    return shared_layout(key)[2]


def draw_qkv(key, part):
    subkeys = jax.random.split(jax.random.fold_in(key, 29), 1)
    base = jnp.clip(jax.random.normal(subkeys[0], (3, TOKENS, WIDTH), jnp.float32), -4.0, 4.0)
    scaled = base * jnp.array([1.0, 1.0, 2.0], jnp.float32)[:, None, None]
    return scaled.astype(jnp.bfloat16)


def draw_cache_uncond(key, part):
    subkeys = jax.random.split(jax.random.fold_in(key, 41), 3)
    row_scale = jnp.exp(jax.random.uniform(subkeys[1], (TOKENS, 1), jnp.float32, -2.302585, 0.0))
    column_scale = jnp.exp(jax.random.uniform(subkeys[2], (1, WIDTH), jnp.float32, -2.302585, 0.0))
    base = jnp.clip(jax.random.normal(subkeys[0], (TOKENS, WIDTH), jnp.float32), -4.0, 4.0)
    return (base * row_scale * column_scale).astype(jnp.bfloat16)


def levels(key, shape, cuts, smallest, high):
    def one(axis_at, shards_of):
        steps = jax.random.uniform(jax.random.fold_in(jax.random.fold_in(key, 6), axis_at), (shards_of,), jnp.float32, smallest / len(cuts), high / len(cuts))
        return jnp.repeat(jnp.exp(steps), shape[axis_at] // shards_of).reshape((-1,) + (1,) * (len(shape) - axis_at - 1))

    factor_of = one(*cuts[0])
    for cut in cuts[1:]:
        factor_of = factor_of * one(*cut)
    return factor_of


def bell_draw(own_key, dims, deviation, limit, cuts=(), kind=jnp.bfloat16):
    drawn = deviation * jax.random.normal(own_key, dims, jnp.float32)
    if cuts:
        drawn = drawn * levels(own_key, dims, cuts, -0.22, 0.18)
    return jnp.clip(drawn, -limit, limit).astype(kind)


def setup_inputs(seed: int = 0) -> dict:
    splits = jax.random.split(jax.random.key(seed), 11)
    qkv = draw_qkv(jax.random.fold_in(splits[10], 71), 0)
    token_rank = draw_token_rank(jax.random.fold_in(splits[10], 71), 0)
    cluster_sizes = draw_cluster_sizes(jax.random.fold_in(splits[10], 71), 0)
    cluster_owner = draw_cluster_owner(jax.random.fold_in(splits[10], 71), 0)
    cache_zero = bell_draw(splits[4], (TOKENS, WIDTH), 0.3, 1.796875, ((0, 16), (1, 2)))
    cache_one = bell_draw(splits[5], (TOKENS, WIDTH), 0.3, 1.796875, ((0, 16), (1, 2)))
    cache_two = bell_draw(splits[6], (TOKENS, WIDTH), 0.3, 1.796875, ((0, 16), (1, 2)))
    cache_uncond = draw_cache_uncond(jax.random.fold_in(splits[10], 71), 0)
    norm_gain = jnp.clip(1.0 + 0.1 * jax.random.normal(splits[8], (WIDTH,), jnp.float32), 0.5, 1.5)
    norm_bias = bell_draw(splits[9], (WIDTH,), 0.5, 3.0, (), jnp.float32)
    return dict(qkv=qkv, token_rank=token_rank, cluster_sizes=cluster_sizes, cluster_owner=cluster_owner, cache_zero=cache_zero, cache_one=cache_one, cache_two=cache_two, cache_uncond=cache_uncond, norm_gain=norm_gain, norm_bias=norm_bias)


guide_scale = 6.0
norm_eps = 1e-05

def group_attention(operands):
    queries, keys_in, values_in, groups, members = operands
    tokens_total = queries.shape[0]
    ordering = jnp.argsort(groups, stable=True).astype(jnp.int32)
    group_sizes = lax.optimization_barrier(jnp.sum((groups[:, None] == jnp.arange(N_TOK, dtype=jnp.int32)[None, :]).astype(jnp.int32), axis=0)).astype(jnp.int32)
    group_starts = (jnp.cumsum(group_sizes) - group_sizes).astype(jnp.int32)
    pad_rows = jnp.zeros((CAP, HEAD_DIM), queries.dtype)
    sorted_q = jnp.concatenate([queries[ordering], pad_rows], axis=0)
    sorted_k = jnp.concatenate([keys_in[ordering], pad_rows], axis=0)
    sorted_v = jnp.concatenate([values_in[ordering], pad_rows], axis=0)
    sorted_members = jnp.concatenate([members[ordering], jnp.full((CAP,), -1, jnp.int32)], axis=0)
    window = jnp.arange(CAP, dtype=jnp.int32)

    def one_group(carry, group_id):
        begin = group_starts[group_id]
        block_q = lax.dynamic_slice_in_dim(sorted_q, begin, CAP, 0)
        block_k = lax.dynamic_slice_in_dim(sorted_k, begin, CAP, 0)
        block_v = lax.dynamic_slice_in_dim(sorted_v, begin, CAP, 0)
        block_members = lax.dynamic_slice_in_dim(sorted_members, begin, CAP, 0)
        scores = lax.dot_general(block_q, block_k, (((1,), (1,)), ((), ())), preferred_element_type=jnp.float32) * (1.0 / math.sqrt(HEAD_DIM))
        allowed = block_members[:, None] == block_members[None, :]
        masked = jnp.where(allowed, scores, -jnp.inf)
        largest = lax.optimization_barrier(jnp.max(masked, axis=1, keepdims=True))
        expo = jnp.where(allowed, jnp.exp(masked - largest), 0.0)
        totals = lax.optimization_barrier(jnp.sum(expo, axis=1, keepdims=True))
        probability = (expo / totals).astype(jnp.bfloat16)
        result = jnp.dot(probability, block_v, preferred_element_type=jnp.float32).astype(jnp.bfloat16)
        result = lax.optimization_barrier(result).astype(jnp.float32)
        valid = window < group_sizes[group_id]
        carry = carry.at[begin + window].add(jnp.where(valid[:, None], result, 0.0))
        return (carry, None)
    start_total = jnp.zeros((tokens_total + CAP, HEAD_DIM), jnp.float32)
    summed = lax.scan(one_group, start_total, jnp.arange(N_TOK, dtype=jnp.int32))[0]
    in_order = summed[:tokens_total]
    return jnp.zeros((tokens_total, HEAD_DIM), jnp.float32).at[ordering].set(in_order)

def head_groups(operands):
    rank_row, ends_row, owner_row = operands
    members = lax.optimization_barrier(jnp.sum((ends_row[None, :] <= rank_row[:, None]).astype(jnp.int32), axis=1)).astype(jnp.int32)
    return (members, owner_row[members])

def reference(qkv, token_rank, cluster_sizes, cluster_owner, cache_zero, cache_one, cache_two, cache_uncond, norm_gain, norm_bias):
    cluster_ends = jnp.cumsum(cluster_sizes, axis=1).astype(jnp.int32)
    members, groups = lax.map(head_groups, (token_rank, cluster_ends, cluster_owner))
    per_head = qkv.reshape(3, TOKENS, HEADS, HEAD_DIM).transpose(0, 2, 1, 3)
    outputs = lax.map(group_attention, (per_head[0], per_head[1], per_head[2], groups, members))
    taylor_zero = outputs.transpose(1, 0, 2).reshape(TOKENS, WIDTH).astype(jnp.bfloat16)
    attention_wide = taylor_zero.astype(jnp.float32)
    first_diff = (attention_wide - cache_zero.astype(jnp.float32)) / STEP_GAP
    second_diff = (first_diff - cache_one.astype(jnp.float32)) / STEP_GAP
    third_diff = (second_diff - cache_two.astype(jnp.float32)) / STEP_GAP
    uncond_wide = cache_uncond.astype(jnp.float32)
    guided = (uncond_wide + guide_scale * (attention_wide - uncond_wide)).astype(jnp.bfloat16)
    widened = lax.optimization_barrier(guided).astype(jnp.float32)
    row_mean = lax.optimization_barrier(jnp.mean(widened, axis=1, keepdims=True))
    centered = widened - row_mean
    row_var = lax.optimization_barrier(jnp.mean(centered * centered, axis=1, keepdims=True))
    normed = (centered * lax.rsqrt(row_var + norm_eps) * norm_gain + norm_bias).astype(jnp.bfloat16)
    return (normed, taylor_zero, first_diff.astype(jnp.bfloat16), second_diff.astype(jnp.bfloat16), third_diff.astype(jnp.bfloat16))
```

```python
import functools
import math

import jax
import jax.numpy as jnp
from jax import lax
from jax.experimental import pallas as pl
from jax.experimental.pallas import tpu as pltpu
from jax.sharding import PartitionSpec as P

HEAD_DIM = 64
LANES = 128
STEP_GAP = 2
GUIDE = 6.0
EPS = 1e-05
F32 = jnp.float32
BF16 = jnp.bfloat16
MESH = pl.DeviceIdType.MESH
NEG = -1e30
SCORE_SCALE = math.log2(math.e) / math.sqrt(HEAD_DIM)


def mm(a, b):
    return jnp.dot(a, b, preferred_element_type=F32)


def mm_nt(a, b):
    return lax.dot_general(a, b, (((1,), (1,)), ((), ())), preferred_element_type=F32)


def iota(shape, axis):
    return lax.broadcasted_iota(jnp.int32, shape, axis)


def exchange_kernel(
    groups,
    head_peers,
    qkv,
    rank,
    sizes,
    owner,
    uncond,
    att_out,
    rows_out,
    send,
    recv,
    back,
    home,
    gsend,
    grecv,
    codes,
    fs,
    fr,
    bs,
    br,
    hs,
    hr,
):
    me = lax.axis_index("tok")
    my_head = lax.axis_index("head")
    heads, toks = rank.shape
    pairs = heads // 2
    nclust = sizes.shape[1]
    slots = send.shape[2]
    half = slots // 2
    total = groups * slots

    barrier = pltpu.get_barrier_semaphore()

    def greet_tok(k, c):
        pl.semaphore_signal(
            barrier, inc=1, device_id={"tok": lax.rem(me + k, groups)}, device_id_type=MESH
        )
        return c

    def greet_head(k, c):
        pl.semaphore_signal(
            barrier,
            inc=1,
            device_id={"head": lax.rem(my_head + k, head_peers)},
            device_id_type=MESH,
        )
        return c

    lax.fori_loop(1, groups, greet_tok, 0)
    lax.fori_loop(1, head_peers, greet_head, 0)

    upto = (iota((nclust, nclust), 1) <= iota((nclust, nclust), 0)).astype(F32).astype(BF16)
    size_all = sizes[...]
    size_hi = (size_all >> 7).astype(F32).astype(BF16)
    size_lo = (size_all & 127).astype(F32).astype(BF16)
    ends = mm_nt(upto, size_hi) * 128.0 + mm_nt(upto, size_lo)
    before = (iota((nclust, nclust), 1) < iota((nclust, nclust), 0)).astype(F32).astype(BF16)
    starts = mm_nt(before, size_hi) * 128.0 + mm_nt(before, size_lo)

    group_iota = iota((groups, nclust), 0)
    members = []
    hits = []
    for h in range(heads):
        ranks = rank[h : h + 1, :].astype(F32)
        passed = ends[:, h : h + 1] <= ranks
        begun = starts[:, h : h + 1] <= ranks
        members.append(jnp.sum(jnp.where(passed, 1.0, 0.0), axis=0, keepdims=True))
        inside = jnp.where(begun, 1.0, 0.0) - jnp.where(passed, 1.0, 0.0)
        owned = jnp.where(group_iota == owner[h : h + 1, :], 1.0, 0.0).astype(BF16)
        hits.append(mm(owned, inside.astype(BF16)))
    all_hits = jnp.concatenate(hits, axis=0)
    earlier_mat = jnp.where(iota((toks, toks), 0) < iota((toks, toks), 1), 1.0, 0.0).astype(BF16)
    earlier = mm(all_hits.astype(BF16), earlier_mat)
    counts = jnp.sum(all_hits, axis=1, keepdims=True)
    group_base = iota((groups, toks), 0).astype(F32)
    slot_rows = []
    codes[...] = jnp.full(codes.shape, -1.0, F32)
    for h in range(heads):
        lo = h * groups
        hit = hits[h]
        place = earlier[lo : lo + groups]
        if h % 2 == 1:
            place = place + counts[lo - groups : lo]
        spot = jnp.sum(hit * place, axis=0, keepdims=True)
        dest = jnp.sum(hit * group_base, axis=0, keepdims=True)
        slot_rows.append((dest * slots + spot).astype(jnp.int32))
        code = dest * half + spot
        codes[h : h + 1, :] = jnp.where(spot < half, code, -1.0)
        codes[heads + h : heads + h + 1, :] = jnp.where(spot >= half, code - half, -1.0)

    lane_tok = iota((toks, LANES), 1)
    slot_iota = iota((total, toks), 0)
    tag_row = iota((LANES, toks), 0)

    def pack(p):
        cols = slice(p * LANES, (p + 1) * LANES)
        q = qkv[0, :, cols].astype(F32)
        k = qkv[1, :, cols].astype(F32)
        v = qkv[2, :, cols].astype(F32)
        first = None
        for side in range(2):
            h = 2 * p + side
            pick = jnp.where(slot_iota == slot_rows[h], 1.0, 0.0).astype(BF16)
            tags = jnp.where(
                tag_row == HEAD_DIM,
                members[h] + 1.0,
                jnp.where(tag_row == HEAD_DIM + 1, float(side), 0.0),
            )
            tag_cols = jnp.transpose(tags)
            if side == 0:
                qv = jnp.where(lane_tok < HEAD_DIM, q, pltpu.roll(v, HEAD_DIM, 1))
                kt = jnp.where(lane_tok < HEAD_DIM, k, tag_cols)
            else:
                qv = jnp.where(lane_tok < HEAD_DIM, pltpu.roll(q, HEAD_DIM, 1), v)
                kt = jnp.where(lane_tok < HEAD_DIM, pltpu.roll(k, HEAD_DIM, 1), tag_cols)
            both = jnp.concatenate([qv, kt], axis=1).astype(BF16)
            part = mm(pick, both)
            first = part if first is None else first + part
        send[p] = first.astype(BF16).reshape(groups, slots, 2 * LANES)

    def forward(p, k):
        dst = lax.rem(me + k, groups)
        return pltpu.make_async_remote_copy(
            src_ref=send.at[p, dst],
            dst_ref=recv.at[p, me],
            send_sem=fs.at[p, dst],
            recv_sem=fr.at[p, me],
            device_id={"tok": dst},
            device_id_type=MESH,
        )

    def forward_wait(p, k):
        src = lax.rem(me + k, groups)
        return pltpu.make_async_remote_copy(
            src_ref=send.at[p, src],
            dst_ref=recv.at[p, src],
            send_sem=fs.at[p, src],
            recv_sem=fr.at[p, src],
            device_id={"tok": src},
            device_id_type=MESH,
        )

    def backward(p, k):
        dst = lax.rem(me + k, groups)
        return pltpu.make_async_remote_copy(
            src_ref=back.at[p, dst],
            dst_ref=home.at[p, me],
            send_sem=bs.at[p, dst],
            recv_sem=br.at[p, me],
            device_id={"tok": dst},
            device_id_type=MESH,
        )

    def backward_wait(p, k):
        src = lax.rem(me + k, groups)
        return pltpu.make_async_remote_copy(
            src_ref=back.at[p, src],
            dst_ref=home.at[p, src],
            send_sem=bs.at[p, src],
            recv_sem=br.at[p, src],
            device_id={"tok": src},
            device_id_type=MESH,
        )

    def loop(count, act):
        def body(k, c):
            act(k)
            return c

        lax.fori_loop(1, count, body, 0)

    for p in range(pairs):
        pack(p)
        if p == 0:
            pl.semaphore_wait(barrier, groups - 1 + head_peers - 1)
        loop(groups, lambda k: forward(p, k).start())
        recv[p, me] = send[p, me]

    code_cols = jnp.transpose(codes[...])
    back_iota = iota((toks, groups * half), 1).astype(F32)

    row_block = min(total, 256)
    wide_lane = iota((total, LANES), 1)
    sel_row = iota((8, LANES), 1)
    sel_r = jnp.where(
        sel_row == HEAD_DIM, 2.0, jnp.where(sel_row == HEAD_DIM + 1, 1.0, 0.0)
    ).astype(BF16)
    sel_col = iota((LANES, LANES), 0)
    sel_c = jnp.where(
        sel_col == HEAD_DIM, 2.0, jnp.where(sel_col == HEAD_DIM + 1, 1.0, 0.0)
    ).astype(BF16)

    for p in range(pairs):
        loop(groups, lambda k: forward_wait(p, k).wait_recv())
        blocks = recv[p].reshape(total, 2 * LANES)
        qv = blocks[:, :LANES]
        kt = blocks[:, LANES:]
        keys = jnp.where(wide_lane < HEAD_DIM, kt.astype(F32), 0.0).astype(BF16)
        tag_r = mm_nt(sel_r, kt)[0:1, :]
        chunk_groups = row_block // slots

        def attend(i, c):
            here = pl.ds(i * chunk_groups, chunk_groups)
            mine = recv[p, here].reshape(row_block, 2 * LANES)
            scores = mm_nt(mine[:, :LANES], keys)
            tag_c = mm(mine[:, LANES:], sel_c)
            tag_c = jnp.concatenate([tag_c] * (total // LANES), axis=1)
            masked = jnp.where(tag_c == tag_r, scores * SCORE_SCALE, NEG)
            largest = jnp.max(masked, axis=1, keepdims=True)
            expo = jnp.exp2(masked - largest)
            scale = 1.0 / jnp.sum(expo, axis=1, keepdims=True)
            out = mm((expo * scale).astype(BF16), qv)
            out = out.reshape(chunk_groups, slots, LANES)
            low = pltpu.roll(out[:, :half].reshape(chunk_groups * half, LANES), HEAD_DIM, 1)
            high = out[:, half:].reshape(chunk_groups * half, LANES)
            lane = iota((chunk_groups * half, LANES), 1)
            packed = jnp.where(lane < HEAD_DIM, low, high).astype(BF16)
            back[p, here] = packed.reshape(chunk_groups, half, LANES)
            return c

        steps = total // row_block
        lax.fori_loop(0, steps, attend, 0, unroll=steps <= 2)
        loop(groups, lambda k: backward(p, k).start())
        home[p, me] = back[p, me]

    peer_rows = toks // head_peers

    def guide(p, k):
        dst = lax.rem(my_head + k, head_peers)
        return pltpu.make_async_remote_copy(
            src_ref=gsend.at[p, dst],
            dst_ref=grecv.at[p, my_head],
            send_sem=hs.at[p, dst],
            recv_sem=hr.at[p, my_head],
            device_id={"head": dst},
            device_id_type=MESH,
        )

    def guide_wait(p, k):
        src = lax.rem(my_head + k, head_peers)
        return pltpu.make_async_remote_copy(
            src_ref=gsend.at[p, src],
            dst_ref=grecv.at[p, src],
            send_sem=hs.at[p, src],
            recv_sem=hr.at[p, src],
            device_id={"head": src},
            device_id_type=MESH,
        )

    for p in range(pairs):
        picks = []
        for h in (2 * p, 2 * p + 1):
            for row in (h, heads + h):
                hit = back_iota == code_cols[:, row : row + 1]
                picks.append(jnp.where(hit, 1.0, 0.0).astype(BF16))
        loop(groups, lambda k: backward_wait(p, k).wait_recv())
        arrived = home[p].reshape(groups * half, LANES)
        a_low, a_high, b_low, b_high = [mm(pick, arrived) for pick in picks]
        left = a_low + pltpu.roll(a_high, HEAD_DIM, 1)
        right = b_high + pltpu.roll(b_low, HEAD_DIM, 1)
        att = jnp.where(lane_tok < HEAD_DIM, left, right)
        cols = slice(p * LANES, (p + 1) * LANES)
        att_out[:, cols] = att.astype(BF16)
        base = uncond[:, cols].astype(F32)
        guided = (base + GUIDE * (att - base)).astype(BF16)
        gsend[p] = guided.reshape(head_peers, peer_rows, LANES)
        loop(head_peers, lambda k: guide(p, k).start())
        grecv[p, my_head] = gsend[p, my_head]

    for p in range(pairs):
        loop(head_peers, lambda k: guide_wait(p, k).wait_recv())
        for src in range(head_peers):
            at = (src * pairs + p) * LANES
            rows_out[:, at : at + LANES] = grecv[p, src]

    for p in range(pairs):
        loop(groups, lambda k: forward_wait(p, k).wait_send())
        loop(groups, lambda k: backward_wait(p, k).wait_send())
        loop(head_peers, lambda k: guide_wait(p, k).wait_send())


def finish_kernel(
    att, rows, zero, one, two, gain, bias, normed, att_out, first_out, second_out, third_out
):
    gap = 1.0 / STEP_GAP
    wide = att[...]
    att_out[...] = wide
    first = (wide.astype(F32) - zero[...].astype(F32)) * gap
    first_out[...] = first.astype(BF16)
    second = (first - one[...].astype(F32)) * gap
    second_out[...] = second.astype(BF16)
    third = (second - two[...].astype(F32)) * gap
    third_out[...] = third.astype(BF16)
    guided = rows[...].astype(F32)
    inv = 1.0 / guided.shape[1]
    centered = guided - jnp.sum(guided, axis=1, keepdims=True) * inv
    var = jnp.sum(centered * centered, axis=1, keepdims=True) * inv
    normed[...] = (centered * lax.rsqrt(var + EPS) * gain[...] + bias[...]).astype(BF16)


def on_device(
    groups,
    head_peers,
    qkv,
    token_rank,
    cluster_sizes,
    cluster_owner,
    cache_zero,
    cache_one,
    cache_two,
    cache_uncond,
    norm_gain,
    norm_bias,
):
    heads, toks = token_rank.shape
    pairs = heads // 2
    width = norm_gain.shape[0]
    mine = cache_zero.shape[1]
    share = 2 * toks // groups
    slots = -(-share // 32) * 32
    half = slots // 2
    peer_rows = toks // head_peers
    vmem = pl.BlockSpec(memory_space=pltpu.VMEM)
    att, rows = pl.pallas_call(
        functools.partial(exchange_kernel, groups, head_peers),
        out_shape=(
            jax.ShapeDtypeStruct((toks, mine), BF16),
            jax.ShapeDtypeStruct((peer_rows, width), BF16),
        ),
        in_specs=[vmem] * 5,
        out_specs=[vmem] * 2,
        scratch_shapes=[
            pltpu.VMEM((pairs, groups, slots, 2 * LANES), BF16),
            pltpu.VMEM((pairs, groups, slots, 2 * LANES), BF16),
            pltpu.VMEM((pairs, groups, half, LANES), BF16),
            pltpu.VMEM((pairs, groups, half, LANES), BF16),
            pltpu.VMEM((pairs, head_peers, peer_rows, LANES), BF16),
            pltpu.VMEM((pairs, head_peers, peer_rows, LANES), BF16),
            pltpu.VMEM((LANES, toks), F32),
            pltpu.SemaphoreType.DMA((pairs, groups)),
            pltpu.SemaphoreType.DMA((pairs, groups)),
            pltpu.SemaphoreType.DMA((pairs, groups)),
            pltpu.SemaphoreType.DMA((pairs, groups)),
            pltpu.SemaphoreType.DMA((pairs, head_peers)),
            pltpu.SemaphoreType.DMA((pairs, head_peers)),
        ],
        compiler_params=pltpu.CompilerParams(
            collective_id=0, has_side_effects=True, vmem_limit_bytes=48 * 1024 * 1024
        ),
        name="exchange",
    )(qkv, token_rank, cluster_sizes, cluster_owner, cache_uncond)
    piece = jax.ShapeDtypeStruct((toks, mine), BF16)
    return pl.pallas_call(
        finish_kernel,
        out_shape=(jax.ShapeDtypeStruct((peer_rows, width), BF16), piece, piece, piece, piece),
        in_specs=[vmem] * 7,
        out_specs=[vmem] * 5,
        compiler_params=pltpu.CompilerParams(vmem_limit_bytes=32 * 1024 * 1024),
        name="finish",
    )(
        att,
        rows,
        cache_zero,
        cache_one,
        cache_two,
        norm_gain.reshape(1, width),
        norm_bias.reshape(1, width),
    )


def solution(mesh):
    sides = P("tok", "head")
    return jax.shard_map(
        functools.partial(on_device, mesh.shape["tok"], mesh.shape["head"]),
        mesh=mesh,
        in_specs=(
            P(None, "tok", "head"),
            P("head", "tok"),
            P("head", None),
            P("head", None),
            sides,
            sides,
            sides,
            sides,
            P(),
            P(),
        ),
        out_specs=(P(("tok", "head"), None), sides, sides, sides, sides),
        check_vma=False,
    )
```

```python
import functools
import math

import jax
import jax.numpy as jnp
from jax import lax
from jax.experimental import pallas as pl
from jax.experimental.pallas import tpu as pltpu
from jax.sharding import PartitionSpec as P

HEAD_DIM = 64
LANES = 128
STEP_GAP = 2
GUIDE = 6.0
EPS = 1e-05
F32 = jnp.float32
BF16 = jnp.bfloat16
MESH = pl.DeviceIdType.MESH
NEG = -1e30
SCORE_SCALE = math.log2(math.e) / math.sqrt(HEAD_DIM)


def mm(a, b):
    return jnp.dot(a, b, preferred_element_type=F32)


def mm_nt(a, b):
    return lax.dot_general(a, b, (((1,), (1,)), ((), ())), preferred_element_type=F32)


def iota(shape, axis):
    return lax.broadcasted_iota(jnp.int32, shape, axis)


def stride_of(groups):
    for step in range(max(groups // 2 - 1, 1), 0, -1):
        if math.gcd(step, groups) == 1:
            return step
    return 1


def loop(count, act):
    def body(k, c):
        act(k)
        return c

    lax.fori_loop(1, count, body, 0)


def exchange_kernel(
    groups,
    head_peers,
    qkv_hbm,
    rank_hbm,
    sizes_hbm,
    owner_hbm,
    uncond_hbm,
    att_hbm,
    rows_hbm,
    qkv,
    rank,
    sizes,
    owner,
    uncond,
    att_out,
    rows_out,
    send,
    recv,
    tag_send,
    tag_recv,
    back,
    home,
    gsend,
    grecv,
    codes,
    fetch,
    store,
    ts,
    tr,
    fs,
    fr,
    bs,
    br,
    hs,
    hr,
):
    me = lax.axis_index("tok")
    my_head = lax.axis_index("head")
    heads, toks = rank.shape
    pairs = heads // 2
    nclust = sizes.shape[1]
    half = back.shape[2]
    slots = 2 * half
    halves = groups * half
    total = groups * slots
    stride = stride_of(groups)

    fetches = [
        pltpu.make_async_copy(src, dst, fetch.at[i])
        for i, (src, dst) in enumerate(
            (
                (sizes_hbm, sizes),
                (owner_hbm, owner),
                (rank_hbm, rank),
                (qkv_hbm, qkv),
                (uncond_hbm, uncond),
            )
        )
    ]
    for one in fetches:
        one.start()

    barrier = pltpu.get_barrier_semaphore()

    def greet(axis, count, mine):
        loop(
            count,
            lambda k: pl.semaphore_signal(
                barrier,
                inc=1,
                device_id={axis: lax.rem(mine + k, count)},
                device_id_type=MESH,
            ),
        )

    greet("tok", groups, me)
    greet("head", head_peers, my_head)

    upto = jnp.where(iota((nclust, nclust), 1) <= iota((nclust, nclust), 0), 1.0, 0.0).astype(BF16)
    before = jnp.where(iota((nclust, nclust), 1) < iota((nclust, nclust), 0), 1.0, 0.0).astype(BF16)
    earlier_mat = jnp.where(iota((toks, toks), 0) < iota((toks, toks), 1), 1.0, 0.0).astype(BF16)
    group_iota = iota((groups, nclust), 0)
    group_base = iota((groups, toks), 0).astype(F32)

    fetches[0].wait()
    size_all = sizes[...]
    size_hi = (size_all >> 7).astype(F32).astype(BF16)
    size_lo = (size_all & 127).astype(F32).astype(BF16)
    ends = mm_nt(upto, size_hi) * 128.0 + mm_nt(upto, size_lo)
    starts = mm_nt(before, size_hi) * 128.0 + mm_nt(before, size_lo)
    fetches[1].wait()
    fetches[2].wait()

    hits = []
    insides = []
    owns = []
    for h in range(heads):
        ranks = rank[h : h + 1, :].astype(F32)
        passed = jnp.where(ends[:, h : h + 1] <= ranks, 1.0, 0.0)
        begun = jnp.where(starts[:, h : h + 1] <= ranks, 1.0, 0.0)
        insides.append((begun - passed).astype(BF16))
        owns.append(jnp.where(group_iota == owner[h : h + 1, :], 1.0, 0.0))
        hits.append(mm(owns[h].astype(BF16), insides[h]))
    all_hits = jnp.concatenate(hits, axis=0)
    earlier = mm(all_hits.astype(BF16), earlier_mat)
    counts = jnp.sum(all_hits, axis=1, keepdims=True)
    slot_rows = []
    spots = []
    codes[...] = jnp.full(codes.shape, -1.0, F32)
    for h in range(heads):
        lo = h * groups
        hit = hits[h]
        place = earlier[lo : lo + groups]
        if h % 2 == 1:
            place = place + counts[lo - groups : lo]
        spot = jnp.sum(hit * place, axis=0, keepdims=True)
        dest = jnp.sum(hit * group_base, axis=0, keepdims=True)
        spots.append(spot)
        slot_rows.append((dest * slots + spot).astype(jnp.int32))
        code = dest * half + spot
        codes[h : h + 1, :] = jnp.where(spot < half, code, -1.0)
        codes[heads + h : heads + h + 1, :] = jnp.where(spot >= half, code - half, -1.0)

    lane_tok = iota((toks, LANES), 1)
    lane_half = iota((halves, LANES), 1)
    slot_iota = iota((total, toks), 0)

    def pack(p):
        cols = slice(p * LANES, (p + 1) * LANES)
        q = qkv[0, :, cols].astype(F32)
        k = qkv[1, :, cols].astype(F32)
        v = qkv[2, :, cols].astype(F32)
        q_turn = pltpu.roll(q, HEAD_DIM, 1)
        k_turn = pltpu.roll(k, HEAD_DIM, 1)
        v_turn = pltpu.roll(v, HEAD_DIM, 1)
        low = lane_tok < HEAD_DIM
        sides = (
            (jnp.where(low, q, k_turn), jnp.where(low, v, v_turn)),
            (jnp.where(low, q_turn, k), jnp.where(low, v_turn, v)),
        )
        out = None
        for side in range(2):
            pick = jnp.where(slot_iota == slot_rows[2 * p + side], 1.0, 0.0).astype(BF16)
            part = mm(pick, jnp.concatenate(sides[side], axis=1).astype(BF16))
            out = part if out is None else out + part
        out = out.reshape(groups, slots, 2 * LANES)
        send[p, :, :slots] = out[:, :, :LANES].astype(BF16)
        v_low = out[:, :half, LANES:].reshape(halves, LANES)
        v_high = out[:, half:, LANES:].reshape(halves, LANES)
        v_both = jnp.where(lane_half < HEAD_DIM, v_low, v_high).astype(BF16)
        send[p, :, slots:] = v_both.reshape(groups, half, LANES)

    def pair_copy(src, dst, src_sem, dst_sem, p, to):
        return pltpu.make_async_remote_copy(
            src_ref=src.at[p, to],
            dst_ref=dst.at[p, me],
            send_sem=src_sem.at[p, to],
            recv_sem=dst_sem.at[p, me],
            device_id={"tok": to},
            device_id_type=MESH,
        )

    def pair_wait(src, dst, src_sem, dst_sem, p, at):
        return pltpu.make_async_remote_copy(
            src_ref=src.at[p, at],
            dst_ref=dst.at[p, at],
            send_sem=src_sem.at[p, at],
            recv_sem=dst_sem.at[p, at],
            device_id={"tok": at},
            device_id_type=MESH,
        )

    def other(k):
        return lax.rem(me + k * stride, groups)

    forward = (send, recv, fs, fr)
    backward = (back, home, bs, br)
    tagged = (tag_send, tag_recv, ts, tr)

    fetches[3].wait()
    for p in range(pairs):
        pack(p)
        if p == 0:
            pl.semaphore_wait(barrier, groups - 1 + head_peers - 1)
        loop(groups, lambda k: pair_copy(*forward, p, other(k)).start())
        recv[p, me] = send[p, me]
        if p == 0:
            lanes = tag_send.shape[3]
            tag_iota = iota((lanes, toks), 0).astype(F32)
            tags = None
            for h in range(heads):
                own = owns[h].astype(BF16)
                ordinal = mm_nt(own, before) + (1.0 + 128.0 * (h % 2))
                value = mm((owns[h] * ordinal).astype(BF16), insides[h]).astype(BF16)
                spread = tag_iota == spots[h] + float((h // 2) * slots)
                part = mm_nt(value, jnp.where(spread, 1.0, 0.0).astype(BF16))
                tags = part if tags is None else tags + part
            tag_send[0] = tags.reshape(groups, 1, lanes)
            loop(groups, lambda k: pair_copy(*tagged, 0, other(k)).start())
            tag_recv[0, me] = tag_send[0, me]

    code_cols = jnp.transpose(codes[...])
    back_iota = iota((toks, halves), 1).astype(F32)

    loop(groups, lambda k: pair_wait(*tagged, 0, other(k)).wait_recv())
    tag_lanes = tag_recv.shape[3]
    tags_in = tag_recv[0].reshape(groups, tag_lanes).astype(BF16)
    order = iota((total, groups), 0)
    source = jnp.where(order >= halves, order - halves, order) // half
    from_source = jnp.where(source == iota((total, groups), 1), 1.0, 0.0).astype(BF16)
    spread_tags = mm(from_source, tags_in)
    order = iota((total, tag_lanes), 0)
    spot_in = jnp.where(order >= halves, order - halves, order) % half + jnp.where(
        order >= halves, half, 0
    )
    tag_lane = iota((total, tag_lanes), 1)
    tag_rows = []
    tag_cols = []
    for p in range(pairs):
        kept = jnp.where(tag_lane == spot_in + p * slots, spread_tags, 0.0)
        tag_cols.append(jnp.sum(kept, axis=1, keepdims=True))
        tag_rows.append(mm_nt(jnp.ones((8, tag_lanes), BF16), kept.astype(BF16))[0:1, :])

    row_block = min(total, 256)
    for p in range(pairs):
        loop(groups, lambda k: pair_wait(*forward, p, other(k)).wait_recv())
        qk = jnp.concatenate(
            [
                recv[p, :, :half].reshape(halves, LANES),
                recv[p, :, half:slots].reshape(halves, LANES),
            ],
            axis=0,
        ).astype(F32)
        wide_lane = iota((total, LANES), 1)
        queries = jnp.where(wide_lane < HEAD_DIM, qk, 0.0).astype(BF16)
        keys = pltpu.roll(qk, HEAD_DIM, 1).astype(BF16)
        v_both = recv[p, :, slots:].reshape(halves, LANES).astype(F32)
        values = jnp.concatenate([v_both, pltpu.roll(v_both, HEAD_DIM, 1)], axis=0).astype(BF16)
        outs = []
        for i in range(total // row_block):
            here = slice(i * row_block, (i + 1) * row_block)
            scores = mm_nt(queries[here], keys)
            same = tag_cols[p][here] == tag_rows[p]
            masked = jnp.where(same, scores * SCORE_SCALE, NEG)
            largest = jnp.max(masked, axis=1, keepdims=True)
            expo = jnp.exp2(masked - largest)
            scale = 1.0 / jnp.sum(expo, axis=1, keepdims=True)
            outs.append(mm((expo * scale).astype(BF16), values))
        out = jnp.concatenate(outs, axis=0)
        packed = jnp.where(
            lane_half < HEAD_DIM, out[:halves], pltpu.roll(out[halves:], HEAD_DIM, 1)
        )
        back[p] = packed.astype(BF16).reshape(groups, half, LANES)
        loop(groups, lambda k: pair_copy(*backward, p, other(k)).start())
        home[p, me] = back[p, me]

    peer_rows = toks // head_peers

    def guide(p, k):
        dst = lax.rem(my_head + k, head_peers)
        return pltpu.make_async_remote_copy(
            src_ref=gsend.at[p, dst],
            dst_ref=grecv.at[p, my_head],
            send_sem=hs.at[p, dst],
            recv_sem=hr.at[p, my_head],
            device_id={"head": dst},
            device_id_type=MESH,
        )

    def guide_wait(p, k):
        src = lax.rem(my_head + k, head_peers)
        return pltpu.make_async_remote_copy(
            src_ref=gsend.at[p, src],
            dst_ref=grecv.at[p, src],
            send_sem=hs.at[p, src],
            recv_sem=hr.at[p, src],
            device_id={"head": src},
            device_id_type=MESH,
        )

    fetches[4].wait()
    for p in range(pairs):
        picks = []
        for h in (2 * p, 2 * p + 1):
            for row in (h, heads + h):
                hit = back_iota == code_cols[:, row : row + 1]
                picks.append(jnp.where(hit, 1.0, 0.0).astype(BF16))
        loop(groups, lambda k: pair_wait(*backward, p, other(k)).wait_recv())
        arrived = home[p].reshape(halves, LANES)
        a_low, a_high, b_low, b_high = [mm(pick, arrived) for pick in picks]
        left = a_low + pltpu.roll(a_high, HEAD_DIM, 1)
        right = b_high + pltpu.roll(b_low, HEAD_DIM, 1)
        att = jnp.where(lane_tok < HEAD_DIM, left, right)
        cols = slice(p * LANES, (p + 1) * LANES)
        att_out[:, cols] = att.astype(BF16)
        base = uncond[:, cols].astype(F32)
        guided = (base + GUIDE * (att - base)).astype(BF16)
        gsend[p] = guided.reshape(head_peers, peer_rows, LANES)
        loop(head_peers, lambda k: guide(p, k).start())
        grecv[p, my_head] = gsend[p, my_head]

    att_store = pltpu.make_async_copy(att_out, att_hbm, store.at[0])
    att_store.start()
    for p in range(pairs):
        loop(head_peers, lambda k: guide_wait(p, k).wait_recv())
        for src in range(head_peers):
            at = (src * pairs + p) * LANES
            rows_out[:, at : at + LANES] = grecv[p, src]
    rows_store = pltpu.make_async_copy(rows_out, rows_hbm, store.at[1])
    rows_store.start()

    loop(groups, lambda k: pair_wait(*tagged, 0, other(k)).wait_send())
    for p in range(pairs):
        loop(groups, lambda k: pair_wait(*forward, p, other(k)).wait_send())
        loop(groups, lambda k: pair_wait(*backward, p, other(k)).wait_send())
        loop(head_peers, lambda k: guide_wait(p, k).wait_send())
    att_store.wait()
    rows_store.wait()


def finish_kernel(
    att_hbm,
    rows_hbm,
    zero,
    one,
    two,
    gain,
    bias,
    normed,
    att_out,
    first_out,
    second_out,
    third_out,
    rows,
    fetch,
):
    att_fetch = pltpu.make_async_copy(att_hbm, att_out, fetch.at[0])
    rows_fetch = pltpu.make_async_copy(rows_hbm, rows, fetch.at[1])
    att_fetch.start()
    rows_fetch.start()
    att_fetch.wait()
    gap = 1.0 / STEP_GAP
    first = (att_out[...].astype(F32) - zero[...].astype(F32)) * gap
    first_out[...] = first.astype(BF16)
    second = (first - one[...].astype(F32)) * gap
    second_out[...] = second.astype(BF16)
    third = (second - two[...].astype(F32)) * gap
    third_out[...] = third.astype(BF16)
    rows_fetch.wait()
    guided = rows[...].astype(F32)
    inv = 1.0 / guided.shape[1]
    centered = guided - jnp.sum(guided, axis=1, keepdims=True) * inv
    var = jnp.sum(centered * centered, axis=1, keepdims=True) * inv
    normed[...] = (centered * lax.rsqrt(var + EPS) * gain[...].reshape(1, -1) + bias[...].reshape(1, -1)).astype(BF16)


def on_device(
    groups,
    head_peers,
    qkv,
    token_rank,
    cluster_sizes,
    cluster_owner,
    cache_zero,
    cache_one,
    cache_two,
    cache_uncond,
    norm_gain,
    norm_bias,
):
    heads, toks = token_rank.shape
    pairs = heads // 2
    width = norm_gain.shape[0]
    mine = cache_zero.shape[1]
    share = 2 * toks // groups
    slots = -(-share // 32) * 32
    half = slots // 2
    tag_lanes = -(-pairs * slots // LANES) * LANES
    peer_rows = toks // head_peers
    vmem = pl.BlockSpec(memory_space=pltpu.VMEM)
    hbm = pl.BlockSpec(memory_space=pltpu.HBM)
    att, rows = pl.pallas_call(
        functools.partial(exchange_kernel, groups, head_peers),
        out_shape=(
            jax.ShapeDtypeStruct((toks, mine), BF16),
            jax.ShapeDtypeStruct((peer_rows, width), BF16),
        ),
        in_specs=[hbm] * 5,
        out_specs=[hbm] * 2,
        scratch_shapes=[
            pltpu.VMEM(qkv.shape, BF16),
            pltpu.VMEM(token_rank.shape, jnp.int32),
            pltpu.VMEM(cluster_sizes.shape, jnp.int32),
            pltpu.VMEM(cluster_owner.shape, jnp.int32),
            pltpu.VMEM(cache_uncond.shape, BF16),
            pltpu.VMEM((toks, mine), BF16),
            pltpu.VMEM((peer_rows, width), BF16),
            pltpu.VMEM((pairs, groups, slots + half, LANES), BF16),
            pltpu.VMEM((pairs, groups, slots + half, LANES), BF16),
            pltpu.VMEM((1, groups, 1, tag_lanes), F32),
            pltpu.VMEM((1, groups, 1, tag_lanes), F32),
            pltpu.VMEM((pairs, groups, half, LANES), BF16),
            pltpu.VMEM((pairs, groups, half, LANES), BF16),
            pltpu.VMEM((pairs, head_peers, peer_rows, LANES), BF16),
            pltpu.VMEM((pairs, head_peers, peer_rows, LANES), BF16),
            pltpu.VMEM((LANES, toks), F32),
            pltpu.SemaphoreType.DMA((5,)),
            pltpu.SemaphoreType.DMA((2,)),
            pltpu.SemaphoreType.DMA((1, groups)),
            pltpu.SemaphoreType.DMA((1, groups)),
            pltpu.SemaphoreType.DMA((pairs, groups)),
            pltpu.SemaphoreType.DMA((pairs, groups)),
            pltpu.SemaphoreType.DMA((pairs, groups)),
            pltpu.SemaphoreType.DMA((pairs, groups)),
            pltpu.SemaphoreType.DMA((pairs, head_peers)),
            pltpu.SemaphoreType.DMA((pairs, head_peers)),
        ],
        compiler_params=pltpu.CompilerParams(
            collective_id=0, has_side_effects=True, vmem_limit_bytes=56 * 1024 * 1024
        ),
        name="exchange",
    )(qkv, token_rank, cluster_sizes, cluster_owner, cache_uncond)
    piece = jax.ShapeDtypeStruct((toks, mine), BF16)
    return pl.pallas_call(
        finish_kernel,
        out_shape=(jax.ShapeDtypeStruct((peer_rows, width), BF16), piece, piece, piece, piece),
        in_specs=[hbm] * 2 + [vmem] * 5,
        out_specs=[vmem] * 5,
        scratch_shapes=[
            pltpu.VMEM((peer_rows, width), BF16),
            pltpu.SemaphoreType.DMA((2,)),
        ],
        compiler_params=pltpu.CompilerParams(vmem_limit_bytes=56 * 1024 * 1024),
        name="finish",
    )(
        att,
        rows,
        cache_zero,
        cache_one,
        cache_two,
        norm_gain,
        norm_bias,
    )


def solution(mesh):
    sides = P("tok", "head")
    return jax.shard_map(
        functools.partial(on_device, mesh.shape["tok"], mesh.shape["head"]),
        mesh=mesh,
        in_specs=(
            P(None, "tok", "head"),
            P("head", "tok"),
            P("head", None),
            P("head", None),
            sides,
            sides,
            sides,
            sides,
            P(),
            P(),
        ),
        out_specs=(P(("tok", "head"), None), sides, sides, sides, sides),
        check_vma=False,
    )
```

```python
import functools
import math

import jax
import jax.numpy as jnp
from jax import lax
from jax.experimental import pallas as pl
from jax.experimental.pallas import tpu as pltpu
from jax.sharding import PartitionSpec as P

HEAD_DIM = 64
LANES = 128
STEP_GAP = 2
GUIDE = 6.0
EPS = 1e-05
F32 = jnp.float32
BF16 = jnp.bfloat16
MESH = pl.DeviceIdType.MESH
NEG = -1e30
SCORE_SCALE = math.log2(math.e) / math.sqrt(HEAD_DIM)


def mm(a, b):
    return jnp.dot(a, b, preferred_element_type=F32)


def mm_nt(a, b):
    return lax.dot_general(a, b, (((1,), (1,)), ((), ())), preferred_element_type=F32)


def iota(shape, axis):
    return lax.broadcasted_iota(jnp.int32, shape, axis)


def stride_of(groups):
    for step in range(max(groups // 2 - 1, 1), 0, -1):
        if math.gcd(step, groups) == 1:
            return step
    return 1


def loop(count, act):
    def body(k, c):
        act(k)
        return c

    lax.fori_loop(1, count, body, 0, unroll=count <= 16)


def exchange_kernel(
    groups,
    head_peers,
    qkv_hbm,
    rank_hbm,
    sizes_hbm,
    owner_hbm,
    uncond_hbm,
    att_hbm,
    rows_hbm,
    qkv,
    rank,
    sizes,
    owner,
    uncond,
    att_out,
    rows_out,
    send,
    recv,
    tag_send,
    tag_recv,
    back,
    home,
    gsend,
    grecv,
    codes,
    fetch,
    store,
    ts,
    tr,
    fs,
    fr,
    bs,
    br,
    hs,
    hr,
):
    me = lax.axis_index("tok")
    my_head = lax.axis_index("head")
    heads, toks = rank.shape
    pairs = heads // 2
    nclust = sizes.shape[1]
    half = back.shape[2]
    slots = 2 * half
    halves = groups * half
    total = groups * slots
    stride = stride_of(groups)

    fetches = [
        pltpu.make_async_copy(src, dst, fetch.at[i])
        for i, (src, dst) in enumerate(
            (
                (sizes_hbm, sizes),
                (owner_hbm, owner),
                (rank_hbm, rank),
                (qkv_hbm, qkv),
                (uncond_hbm, uncond),
            )
        )
    ]
    for one in fetches:
        one.start()

    barrier = pltpu.get_barrier_semaphore()

    def greet(axis, count, mine):
        loop(
            count,
            lambda k: pl.semaphore_signal(
                barrier,
                inc=1,
                device_id={axis: lax.rem(mine + k, count)},
                device_id_type=MESH,
            ),
        )

    greet("tok", groups, me)
    greet("head", head_peers, my_head)

    upto = jnp.where(iota((nclust, nclust), 1) <= iota((nclust, nclust), 0), 1.0, 0.0).astype(BF16)
    before = jnp.where(iota((nclust, nclust), 1) < iota((nclust, nclust), 0), 1.0, 0.0).astype(BF16)
    earlier_mat = jnp.where(iota((toks, toks), 0) < iota((toks, toks), 1), 1.0, 0.0).astype(BF16)
    group_iota = iota((groups, nclust), 0)
    group_base = iota((groups, toks), 0).astype(F32)

    fetches[0].wait()
    size_all = sizes[...]
    size_hi = (size_all >> 7).astype(F32).astype(BF16)
    size_lo = (size_all & 127).astype(F32).astype(BF16)
    ends = mm_nt(upto, size_hi) * 128.0 + mm_nt(upto, size_lo)
    starts = mm_nt(before, size_hi) * 128.0 + mm_nt(before, size_lo)
    fetches[1].wait()
    fetches[2].wait()

    hits = []
    insides = []
    owns = []
    for h in range(heads):
        ranks = rank[h : h + 1, :].astype(F32)
        passed = jnp.where(ends[:, h : h + 1] <= ranks, 1.0, 0.0)
        begun = jnp.where(starts[:, h : h + 1] <= ranks, 1.0, 0.0)
        insides.append((begun - passed).astype(BF16))
        owns.append(jnp.where(group_iota == owner[h : h + 1, :], 1.0, 0.0))
        hits.append(mm(owns[h].astype(BF16), insides[h]))
    all_hits = jnp.concatenate(hits, axis=0)
    earlier = mm(all_hits.astype(BF16), earlier_mat)
    counts = jnp.sum(all_hits, axis=1, keepdims=True)
    slot_rows = []
    spots = []
    codes[...] = jnp.full(codes.shape, -1.0, F32)
    for h in range(heads):
        lo = h * groups
        hit = hits[h]
        place = earlier[lo : lo + groups]
        if h % 2 == 1:
            place = place + counts[lo - groups : lo]
        spot = jnp.sum(hit * place, axis=0, keepdims=True)
        dest = jnp.sum(hit * group_base, axis=0, keepdims=True)
        spots.append(spot)
        slot_rows.append((dest * slots + spot).astype(jnp.int32))
        code = dest * half + spot
        codes[h : h + 1, :] = jnp.where(spot < half, code, -1.0)
        codes[heads + h : heads + h + 1, :] = jnp.where(spot >= half, code - half, -1.0)

    lane_tok = iota((toks, LANES), 1)
    lane_half = iota((halves, LANES), 1)
    slot_iota = iota((total, toks), 0)

    def pack(p):
        cols = slice(p * LANES, (p + 1) * LANES)
        q = qkv[0, :, cols].astype(F32)
        k = qkv[1, :, cols].astype(F32)
        v = qkv[2, :, cols].astype(F32)
        q_turn = pltpu.roll(q, HEAD_DIM, 1)
        k_turn = pltpu.roll(k, HEAD_DIM, 1)
        v_turn = pltpu.roll(v, HEAD_DIM, 1)
        low = lane_tok < HEAD_DIM
        sides = (
            (jnp.where(low, q, k_turn), jnp.where(low, v, v_turn)),
            (jnp.where(low, q_turn, k), jnp.where(low, v_turn, v)),
        )
        out = None
        for side in range(2):
            pick = jnp.where(slot_iota == slot_rows[2 * p + side], 1.0, 0.0).astype(BF16)
            part = mm(pick, jnp.concatenate(sides[side], axis=1).astype(BF16))
            out = part if out is None else out + part
        out = out.reshape(groups, slots, 2 * LANES)
        send[p, :, :slots] = out[:, :, :LANES].astype(BF16)
        v_low = out[:, :half, LANES:].reshape(halves, LANES)
        v_high = out[:, half:, LANES:].reshape(halves, LANES)
        v_both = jnp.where(lane_half < HEAD_DIM, v_low, v_high).astype(BF16)
        send[p, :, slots:] = v_both.reshape(groups, half, LANES)

    def pair_copy(src, dst, src_sem, dst_sem, p, to):
        return pltpu.make_async_remote_copy(
            src_ref=src.at[p, to],
            dst_ref=dst.at[p, me],
            send_sem=src_sem.at[p],
            recv_sem=dst_sem.at[p],
            device_id={"tok": to},
            device_id_type=MESH,
        )

    def pair_wait(src, dst, src_sem, dst_sem, p):
        rest = pl.ds(0, groups - 1)
        return pltpu.make_async_remote_copy(
            src_ref=src.at[p, rest],
            dst_ref=dst.at[p, rest],
            send_sem=src_sem.at[p],
            recv_sem=dst_sem.at[p],
            device_id={"tok": other(1)},
            device_id_type=MESH,
        )

    def other(k):
        return lax.rem(me + k * stride, groups)

    forward = (send, recv, fs, fr)
    backward = (back, home, bs, br)
    tagged = (tag_send, tag_recv, ts, tr)

    fetches[3].wait()
    for p in range(pairs):
        pack(p)
        if p == 0:
            pl.semaphore_wait(barrier, groups - 1 + head_peers - 1)
        loop(groups, lambda k: pair_copy(*forward, p, other(k)).start())
        recv[p, me] = send[p, me]
        if p == 0:
            lanes = tag_send.shape[3]
            tag_iota = iota((lanes, toks), 0).astype(F32)
            tags = None
            for h in range(heads):
                own = owns[h].astype(BF16)
                ordinal = mm_nt(own, before) + (1.0 + 128.0 * (h % 2))
                value = mm((owns[h] * ordinal).astype(BF16), insides[h]).astype(BF16)
                spread = tag_iota == spots[h] + float((h // 2) * slots)
                part = mm_nt(value, jnp.where(spread, 1.0, 0.0).astype(BF16))
                tags = part if tags is None else tags + part
            tag_send[0] = tags.reshape(groups, 1, lanes)
            loop(groups, lambda k: pair_copy(*tagged, 0, other(k)).start())
            tag_recv[0, me] = tag_send[0, me]

    code_cols = jnp.transpose(codes[...])
    back_iota = iota((toks, halves), 1).astype(F32)

    pair_wait(*tagged, 0).wait_recv()
    tag_lanes = tag_recv.shape[3]
    tags_in = tag_recv[0].reshape(groups, tag_lanes).astype(BF16)
    order = iota((total, groups), 0)
    source = jnp.where(order >= halves, order - halves, order) // half
    from_source = jnp.where(source == iota((total, groups), 1), 1.0, 0.0).astype(BF16)
    spread_tags = mm(from_source, tags_in)
    order = iota((total, tag_lanes), 0)
    spot_in = jnp.where(order >= halves, order - halves, order) % half + jnp.where(
        order >= halves, half, 0
    )
    tag_lane = iota((total, tag_lanes), 1)
    tag_rows = []
    tag_cols = []
    for p in range(pairs):
        kept = jnp.where(tag_lane == spot_in + p * slots, spread_tags, 0.0)
        tag_cols.append(jnp.sum(kept, axis=1, keepdims=True))
        tag_rows.append(mm_nt(jnp.ones((8, tag_lanes), BF16), kept.astype(BF16))[0:1, :])

    row_block = min(total, 256)
    for p in range(pairs):
        pair_wait(*forward, p).wait_recv()
        qk = jnp.concatenate(
            [
                recv[p, :, :half].reshape(halves, LANES),
                recv[p, :, half:slots].reshape(halves, LANES),
            ],
            axis=0,
        ).astype(F32)
        wide_lane = iota((total, LANES), 1)
        queries = jnp.where(wide_lane < HEAD_DIM, qk, 0.0).astype(BF16)
        keys = pltpu.roll(qk, HEAD_DIM, 1).astype(BF16)
        v_both = recv[p, :, slots:].reshape(halves, LANES).astype(F32)
        values = jnp.concatenate([v_both, pltpu.roll(v_both, HEAD_DIM, 1)], axis=0).astype(BF16)
        outs = []
        for i in range(total // row_block):
            here = slice(i * row_block, (i + 1) * row_block)
            scores = mm_nt(queries[here], keys)
            same = tag_cols[p][here] == tag_rows[p]
            masked = jnp.where(same, scores * SCORE_SCALE, NEG)
            largest = jnp.max(masked, axis=1, keepdims=True)
            expo = jnp.exp2(masked - largest)
            scale = 1.0 / jnp.sum(expo, axis=1, keepdims=True)
            outs.append(mm((expo * scale).astype(BF16), values))
        out = jnp.concatenate(outs, axis=0)
        packed = jnp.where(
            lane_half < HEAD_DIM, out[:halves], pltpu.roll(out[halves:], HEAD_DIM, 1)
        )
        back[p] = packed.astype(BF16).reshape(groups, half, LANES)
        loop(groups, lambda k: pair_copy(*backward, p, other(k)).start())
        home[p, me] = back[p, me]

    peer_rows = toks // head_peers

    def guide(p, k):
        dst = lax.rem(my_head + k, head_peers)
        return pltpu.make_async_remote_copy(
            src_ref=gsend.at[p, dst],
            dst_ref=grecv.at[p, my_head],
            send_sem=hs.at[p, dst],
            recv_sem=hr.at[p, my_head],
            device_id={"head": dst},
            device_id_type=MESH,
        )

    def guide_wait(p, k):
        src = lax.rem(my_head + k, head_peers)
        return pltpu.make_async_remote_copy(
            src_ref=gsend.at[p, src],
            dst_ref=grecv.at[p, src],
            send_sem=hs.at[p, src],
            recv_sem=hr.at[p, src],
            device_id={"head": src},
            device_id_type=MESH,
        )

    pair_wait(*tagged, 0).wait_send()
    for p in range(pairs):
        pair_wait(*forward, p).wait_send()
    fetches[4].wait()
    for p in range(pairs):
        picks = []
        for h in (2 * p, 2 * p + 1):
            for row in (h, heads + h):
                hit = back_iota == code_cols[:, row : row + 1]
                picks.append(jnp.where(hit, 1.0, 0.0).astype(BF16))
        pair_wait(*backward, p).wait_recv()
        arrived = home[p].reshape(halves, LANES)
        a_low, a_high, b_low, b_high = [mm(pick, arrived) for pick in picks]
        left = a_low + pltpu.roll(a_high, HEAD_DIM, 1)
        right = b_high + pltpu.roll(b_low, HEAD_DIM, 1)
        att = jnp.where(lane_tok < HEAD_DIM, left, right)
        cols = slice(p * LANES, (p + 1) * LANES)
        att_out[:, cols] = att.astype(BF16)
        base = uncond[:, cols].astype(F32)
        guided = (base + GUIDE * (att - base)).astype(BF16)
        gsend[p] = guided.reshape(head_peers, peer_rows, LANES)
        loop(head_peers, lambda k: guide(p, k).start())
        grecv[p, my_head] = gsend[p, my_head]

    att_store = pltpu.make_async_copy(att_out, att_hbm, store.at[0])
    att_store.start()
    for p in range(pairs):
        pair_wait(*backward, p).wait_send()
    for p in range(pairs):
        loop(head_peers, lambda k: guide_wait(p, k).wait_recv())
        for src in range(head_peers):
            at = (src * pairs + p) * LANES
            rows_out[:, at : at + LANES] = grecv[p, src]
    rows_store = pltpu.make_async_copy(rows_out, rows_hbm, store.at[1])
    rows_store.start()

    for p in range(pairs):
        loop(head_peers, lambda k: guide_wait(p, k).wait_send())
    att_store.wait()
    rows_store.wait()


def finish_kernel(
    att_hbm,
    rows_hbm,
    zero_hbm,
    one_hbm,
    two_hbm,
    gain_hbm,
    bias_hbm,
    normed_hbm,
    att_out_hbm,
    first_hbm,
    second_hbm,
    third_hbm,
    att,
    zero,
    one,
    two,
    rows,
    gain,
    bias,
    first_out,
    second_out,
    third_out,
    normed,
    fetch,
    store,
):
    sources = (att_hbm, zero_hbm, one_hbm, two_hbm, rows_hbm, gain_hbm, bias_hbm)
    targets = (att, zero, one, two, rows, gain, bias)
    fetches = [
        pltpu.make_async_copy(src, dst, fetch.at[i])
        for i, (src, dst) in enumerate(zip(sources, targets))
    ]
    for one_fetch in fetches:
        one_fetch.start()
    stores = []

    def put(src, dst):
        copy = pltpu.make_async_copy(src, dst, store.at[len(stores)])
        copy.start()
        stores.append(copy)

    gap = 1.0 / STEP_GAP
    fetches[0].wait()
    put(att, att_out_hbm)
    fetches[1].wait()
    first = (att[...].astype(F32) - zero[...].astype(F32)) * gap
    first_out[...] = first.astype(BF16)
    put(first_out, first_hbm)
    fetches[2].wait()
    second = (first - one[...].astype(F32)) * gap
    second_out[...] = second.astype(BF16)
    put(second_out, second_hbm)
    fetches[3].wait()
    third = (second - two[...].astype(F32)) * gap
    third_out[...] = third.astype(BF16)
    put(third_out, third_hbm)
    for i in (4, 5, 6):
        fetches[i].wait()
    guided = rows[...].astype(F32)
    inv = 1.0 / guided.shape[1]
    centered = guided - jnp.sum(guided, axis=1, keepdims=True) * inv
    var = jnp.sum(centered * centered, axis=1, keepdims=True) * inv
    scaled = centered * lax.rsqrt(var + EPS) * gain[...].reshape(1, -1)
    normed[...] = (scaled + bias[...].reshape(1, -1)).astype(BF16)
    put(normed, normed_hbm)
    for one_store in stores:
        one_store.wait()


def on_device(
    groups,
    head_peers,
    qkv,
    token_rank,
    cluster_sizes,
    cluster_owner,
    cache_zero,
    cache_one,
    cache_two,
    cache_uncond,
    norm_gain,
    norm_bias,
):
    heads, toks = token_rank.shape
    pairs = heads // 2
    width = norm_gain.shape[0]
    mine = cache_zero.shape[1]
    share = 2 * toks // groups
    slots = -(-share // 32) * 32
    half = slots // 2
    tag_lanes = -(-pairs * slots // LANES) * LANES
    peer_rows = toks // head_peers
    hbm = pl.BlockSpec(memory_space=pltpu.HBM)
    att, rows = pl.pallas_call(
        functools.partial(exchange_kernel, groups, head_peers),
        out_shape=(
            jax.ShapeDtypeStruct((toks, mine), BF16),
            jax.ShapeDtypeStruct((peer_rows, width), BF16),
        ),
        in_specs=[hbm] * 5,
        out_specs=[hbm] * 2,
        scratch_shapes=[
            pltpu.VMEM(qkv.shape, BF16),
            pltpu.VMEM(token_rank.shape, jnp.int32),
            pltpu.VMEM(cluster_sizes.shape, jnp.int32),
            pltpu.VMEM(cluster_owner.shape, jnp.int32),
            pltpu.VMEM(cache_uncond.shape, BF16),
            pltpu.VMEM((toks, mine), BF16),
            pltpu.VMEM((peer_rows, width), BF16),
            pltpu.VMEM((pairs, groups, slots + half, LANES), BF16),
            pltpu.VMEM((pairs, groups, slots + half, LANES), BF16),
            pltpu.VMEM((1, groups, 1, tag_lanes), F32),
            pltpu.VMEM((1, groups, 1, tag_lanes), F32),
            pltpu.VMEM((pairs, groups, half, LANES), BF16),
            pltpu.VMEM((pairs, groups, half, LANES), BF16),
            pltpu.VMEM((pairs, head_peers, peer_rows, LANES), BF16),
            pltpu.VMEM((pairs, head_peers, peer_rows, LANES), BF16),
            pltpu.VMEM((LANES, toks), F32),
            pltpu.SemaphoreType.DMA((5,)),
            pltpu.SemaphoreType.DMA((2,)),
            pltpu.SemaphoreType.DMA((1,)),
            pltpu.SemaphoreType.DMA((1,)),
            pltpu.SemaphoreType.DMA((pairs,)),
            pltpu.SemaphoreType.DMA((pairs,)),
            pltpu.SemaphoreType.DMA((pairs,)),
            pltpu.SemaphoreType.DMA((pairs,)),
            pltpu.SemaphoreType.DMA((pairs, head_peers)),
            pltpu.SemaphoreType.DMA((pairs, head_peers)),
        ],
        compiler_params=pltpu.CompilerParams(
            collective_id=0, has_side_effects=True, vmem_limit_bytes=56 * 1024 * 1024
        ),
        name="exchange",
    )(qkv, token_rank, cluster_sizes, cluster_owner, cache_uncond)
    piece = jax.ShapeDtypeStruct((toks, mine), BF16)
    return pl.pallas_call(
        finish_kernel,
        out_shape=(jax.ShapeDtypeStruct((peer_rows, width), BF16), piece, piece, piece, piece),
        in_specs=[hbm] * 7,
        out_specs=[hbm] * 5,
        scratch_shapes=[
            *[pltpu.VMEM((toks, mine), BF16)] * 4,
            pltpu.VMEM((peer_rows, width), BF16),
            pltpu.VMEM((width,), F32),
            pltpu.VMEM((width,), F32),
            *[pltpu.VMEM((toks, mine), BF16)] * 3,
            pltpu.VMEM((peer_rows, width), BF16),
            pltpu.SemaphoreType.DMA((7,)),
            pltpu.SemaphoreType.DMA((5,)),
        ],
        compiler_params=pltpu.CompilerParams(vmem_limit_bytes=56 * 1024 * 1024),
        name="finish",
    )(
        att,
        rows,
        cache_zero,
        cache_one,
        cache_two,
        norm_gain,
        norm_bias,
    )


def solution(mesh):
    sides = P("tok", "head")
    return jax.shard_map(
        functools.partial(on_device, mesh.shape["tok"], mesh.shape["head"]),
        mesh=mesh,
        in_specs=(
            P(None, "tok", "head"),
            P("head", "tok"),
            P("head", None),
            P("head", None),
            sides,
            sides,
            sides,
            sides,
            P(),
            P(),
        ),
        out_specs=(P(("tok", "head"), None), sides, sides, sides, sides),
        check_vma=False,
    )
```

```python
import functools
import math

import jax
import jax.numpy as jnp
from jax import lax
from jax.experimental import pallas as pl
from jax.experimental.pallas import tpu as pltpu
from jax.sharding import PartitionSpec as P

HEAD_DIM = 64
LANES = 128
STEP_GAP = 2
GUIDE = 6.0
EPS = 1e-05
F32 = jnp.float32
BF16 = jnp.bfloat16
MESH = pl.DeviceIdType.MESH
NEG = -1e30
SCORE_SCALE = math.log2(math.e) / math.sqrt(HEAD_DIM)


def mm(a, b):
    return jnp.dot(a, b, preferred_element_type=F32)


def mm_nt(a, b):
    return lax.dot_general(a, b, (((1,), (1,)), ((), ())), preferred_element_type=F32)


def iota(shape, axis):
    return lax.broadcasted_iota(jnp.int32, shape, axis)


def stride_of(groups):
    for step in range(max(groups // 2 - 1, 1), 0, -1):
        if math.gcd(step, groups) == 1:
            return step
    return 1


def loop(count, act):
    def body(k, c):
        act(k)
        return c

    lax.fori_loop(1, count, body, 0, unroll=count <= 16)


def exchange_kernel(
    groups,
    head_peers,
    qkv_hbm,
    rank_hbm,
    sizes_hbm,
    owner_hbm,
    uncond_hbm,
    att_hbm,
    rows_hbm,
    qkv,
    rank,
    sizes,
    owner,
    uncond,
    att_out,
    send,
    recv,
    tag_send,
    tag_recv,
    back,
    home,
    gsend,
    codes,
    tag_cols,
    fetch,
    store,
    ts,
    tr,
    fs,
    fr,
    bs,
    br,
    hs,
    hr,
):
    me = lax.axis_index("tok")
    my_head = lax.axis_index("head")
    heads, toks = rank.shape
    pairs = heads // 2
    nclust = sizes.shape[1]
    half = back.shape[2]
    slots = 2 * half
    halves = groups * half
    total = groups * slots
    stride = stride_of(groups)
    chunk = tag_cols.shape[1] // slots
    steps = groups // chunk
    row_block = chunk * slots

    fetches = [
        pltpu.make_async_copy(src, dst, fetch.at[i])
        for i, (src, dst) in enumerate(
            (
                (sizes_hbm, sizes),
                (owner_hbm, owner),
                (rank_hbm, rank),
                (qkv_hbm, qkv),
                (uncond_hbm, uncond),
            )
        )
    ]
    for one in fetches:
        one.start()

    barrier = pltpu.get_barrier_semaphore()

    def greet(axis, count, mine):
        loop(
            count,
            lambda k: pl.semaphore_signal(
                barrier,
                inc=1,
                device_id={axis: lax.rem(mine + k, count)},
                device_id_type=MESH,
            ),
        )

    greet("tok", groups, me)
    greet("head", head_peers, my_head)

    upto = jnp.where(iota((nclust, nclust), 1) <= iota((nclust, nclust), 0), 1.0, 0.0).astype(BF16)
    before = jnp.where(iota((nclust, nclust), 1) < iota((nclust, nclust), 0), 1.0, 0.0).astype(BF16)
    earlier_mat = jnp.where(iota((toks, toks), 0) < iota((toks, toks), 1), 1.0, 0.0).astype(BF16)
    group_iota = iota((groups, nclust), 0)
    group_base = iota((groups, toks), 0).astype(F32)

    fetches[0].wait()
    size_all = sizes[...]
    size_hi = (size_all >> 7).astype(F32).astype(BF16)
    size_lo = (size_all & 127).astype(F32).astype(BF16)
    ends = mm_nt(upto, size_hi) * 128.0 + mm_nt(upto, size_lo)
    starts = mm_nt(before, size_hi) * 128.0 + mm_nt(before, size_lo)
    fetches[1].wait()
    fetches[2].wait()

    hits = []
    insides = []
    owns = []
    for h in range(heads):
        ranks = rank[h : h + 1, :].astype(F32)
        passed = jnp.where(ends[:, h : h + 1] <= ranks, 1.0, 0.0)
        begun = jnp.where(starts[:, h : h + 1] <= ranks, 1.0, 0.0)
        insides.append((begun - passed).astype(BF16))
        owns.append(jnp.where(group_iota == owner[h : h + 1, :], 1.0, 0.0))
        hits.append(mm(owns[h].astype(BF16), insides[h]))
    all_hits = jnp.concatenate(hits, axis=0)
    earlier = mm(all_hits.astype(BF16), earlier_mat)
    counts = jnp.sum(all_hits, axis=1, keepdims=True)
    slot_rows = []
    spots = []
    codes[...] = jnp.full(codes.shape, -1.0, F32)
    for h in range(heads):
        lo = h * groups
        hit = hits[h]
        place = earlier[lo : lo + groups]
        if h % 2 == 1:
            place = place + counts[lo - groups : lo]
        spot = jnp.sum(hit * place, axis=0, keepdims=True)
        dest = jnp.sum(hit * group_base, axis=0, keepdims=True)
        spots.append(spot)
        slot_rows.append((dest * slots + spot).astype(jnp.int32))
        code = dest * half + spot
        codes[h : h + 1, :] = jnp.where(spot < half, code, -1.0)
        codes[heads + h : heads + h + 1, :] = jnp.where(spot >= half, code - half, -1.0)

    lane_tok = iota((toks, LANES), 1)
    lane_half = iota((halves, LANES), 1)
    slot_iota = iota((total, toks), 0)

    def pack(p):
        cols = slice(p * LANES, (p + 1) * LANES)
        q = qkv[0, :, cols].astype(F32)
        k = qkv[1, :, cols].astype(F32)
        v = qkv[2, :, cols].astype(F32)
        q_turn = pltpu.roll(q, HEAD_DIM, 1)
        k_turn = pltpu.roll(k, HEAD_DIM, 1)
        v_turn = pltpu.roll(v, HEAD_DIM, 1)
        low = lane_tok < HEAD_DIM
        sides = (
            (jnp.where(low, q, k_turn), jnp.where(low, v, v_turn)),
            (jnp.where(low, q_turn, k), jnp.where(low, v_turn, v)),
        )
        out = None
        for side in range(2):
            pick = jnp.where(slot_iota == slot_rows[2 * p + side], 1.0, 0.0).astype(BF16)
            part = mm(pick, jnp.concatenate(sides[side], axis=1).astype(BF16))
            out = part if out is None else out + part
        out = out.reshape(groups, slots, 2 * LANES)
        send[p, :, :slots] = out[:, :, :LANES].astype(BF16)
        v_low = out[:, :half, LANES:].reshape(halves, LANES)
        v_high = out[:, half:, LANES:].reshape(halves, LANES)
        v_both = jnp.where(lane_half < HEAD_DIM, v_low, v_high).astype(BF16)
        send[p, :, slots:] = v_both.reshape(groups, half, LANES)

    def pair_copy(src, dst, src_sem, dst_sem, p, to):
        return pltpu.make_async_remote_copy(
            src_ref=src.at[p, to],
            dst_ref=dst.at[p, me],
            send_sem=src_sem.at[p],
            recv_sem=dst_sem.at[p],
            device_id={"tok": to},
            device_id_type=MESH,
        )

    def pair_wait(src, dst, src_sem, dst_sem, p):
        rest = pl.ds(0, groups - 1)
        return pltpu.make_async_remote_copy(
            src_ref=src.at[p, rest],
            dst_ref=dst.at[p, rest],
            send_sem=src_sem.at[p],
            recv_sem=dst_sem.at[p],
            device_id={"tok": other(1)},
            device_id_type=MESH,
        )

    def other(k):
        return lax.rem(me + k * stride, groups)

    forward = (send, recv, fs, fr)
    backward = (back, home, bs, br)
    tagged = (tag_send, tag_recv, ts, tr)

    fetches[3].wait()
    for p in range(pairs):
        pack(p)
        if p == 0:
            pl.semaphore_wait(barrier, groups - 1 + head_peers - 1)
        loop(groups, lambda k: pair_copy(*forward, p, other(k)).start())
        recv[p, me] = send[p, me]
        if p == 0:
            lanes = tag_send.shape[3]
            tag_iota = iota((lanes, toks), 0).astype(F32)
            tags = None
            for h in range(heads):
                own = owns[h].astype(BF16)
                ordinal = mm_nt(own, before) + (1.0 + 128.0 * (h % 2))
                value = mm((owns[h] * ordinal).astype(BF16), insides[h]).astype(BF16)
                spread = tag_iota == spots[h] + float((h // 2) * slots)
                part = mm_nt(value, jnp.where(spread, 1.0, 0.0).astype(BF16))
                tags = part if tags is None else tags + part
            tag_send[0] = tags.reshape(groups, 1, lanes)
            loop(groups, lambda k: pair_copy(*tagged, 0, other(k)).start())
            tag_recv[0, me] = tag_send[0, me]

    code_cols = jnp.transpose(codes[...])
    back_iota = iota((toks, halves), 1).astype(F32)

    pair_wait(*tagged, 0).wait_recv()
    tag_lanes = tag_recv.shape[3]
    tags_in = tag_recv[0].reshape(groups, tag_lanes).astype(BF16)
    order = iota((total, 1), 0)
    upper = order >= halves
    inner = jnp.where(upper, order - halves, order)
    lane_tags = iota((total, tag_lanes), 1)

    def spread(source, spot, p):
        from_source = jnp.where(source == iota((total, groups), 1), 1.0, 0.0).astype(BF16)
        return jnp.where(lane_tags == spot + p * slots, mm(from_source, tags_in), 0.0)

    tag_rows = []
    for p in range(pairs):
        kept = spread(inner // half, inner % half + jnp.where(upper, half, 0), p)
        tag_rows.append(mm_nt(jnp.ones((8, tag_lanes), BF16), kept.astype(BF16))[0:1, :])
        kept = spread(order // slots, order % slots, p)
        column = jnp.sum(kept, axis=1, keepdims=True)
        tag_cols[p * steps : (p + 1) * steps] = column.reshape(steps, row_block, 1)

    for p in range(pairs):
        pair_wait(*forward, p).wait_recv()
        qk = jnp.concatenate(
            [
                recv[p, :, :half].reshape(halves, LANES),
                recv[p, :, half:slots].reshape(halves, LANES),
            ],
            axis=0,
        ).astype(F32)
        keys = pltpu.roll(qk, HEAD_DIM, 1).astype(BF16)
        v_both = recv[p, :, slots:].reshape(halves, LANES).astype(F32)
        values = jnp.concatenate([v_both, pltpu.roll(v_both, HEAD_DIM, 1)], axis=0).astype(BF16)
        lane_row = iota((row_block, LANES), 1)
        lane_out = iota((chunk * half, LANES), 1)

        def attend(i, c):
            block = lax.rem(lax.div(me, chunk) + 1 + i, steps)
            base = block * chunk
            mine = recv[p, pl.ds(base, chunk), :slots].reshape(row_block, LANES).astype(F32)
            queries = jnp.where(lane_row < HEAD_DIM, mine, 0.0).astype(BF16)
            scores = mm_nt(queries, keys)
            same = tag_cols[p * steps + block] == tag_rows[p]
            masked = jnp.where(same, scores * SCORE_SCALE, NEG)
            largest = jnp.max(masked, axis=1, keepdims=True)
            expo = jnp.exp2(masked - largest)
            scale = 1.0 / jnp.sum(expo, axis=1, keepdims=True)
            out = mm((expo * scale).astype(BF16), values).reshape(chunk, slots, LANES)
            low = out[:, :half].reshape(chunk * half, LANES)
            high = pltpu.roll(out[:, half:].reshape(chunk * half, LANES), HEAD_DIM, 1)
            packed = jnp.where(lane_out < HEAD_DIM, low, high).astype(BF16)
            back[p, pl.ds(base, chunk)] = packed.reshape(chunk, half, LANES)

            def give(j, c):
                to = base + lax.rem(me + j, chunk)

                @pl.when(to != me)
                def _():
                    pair_copy(*backward, p, to).start()

                return c

            lax.fori_loop(0, chunk, give, 0, unroll=steps <= 2)
            return c

        lax.fori_loop(0, steps, attend, 0, unroll=steps <= 2)
        home[p, me] = back[p, me]

    peer_rows = toks // head_peers

    def guide(p, k):
        dst = lax.rem(my_head + k, head_peers)
        return pltpu.make_async_remote_copy(
            src_ref=gsend.at[p, dst],
            dst_ref=rows_hbm.at[my_head, p],
            send_sem=hs.at[p, dst],
            recv_sem=hr.at[p, my_head],
            device_id={"head": dst},
            device_id_type=MESH,
        )

    def guide_wait(p, k):
        src = lax.rem(my_head + k, head_peers)
        return pltpu.make_async_remote_copy(
            src_ref=gsend.at[p, src],
            dst_ref=rows_hbm.at[src, p],
            send_sem=hs.at[p, src],
            recv_sem=hr.at[p, src],
            device_id={"head": src},
            device_id_type=MESH,
        )

    pair_wait(*tagged, 0).wait_send()
    for p in range(pairs):
        pair_wait(*forward, p).wait_send()
    fetches[4].wait()
    keeps = []
    for p in range(pairs):
        picks = []
        for h in (2 * p, 2 * p + 1):
            for row in (h, heads + h):
                hit = back_iota == code_cols[:, row : row + 1]
                picks.append(jnp.where(hit, 1.0, 0.0).astype(BF16))
        pair_wait(*backward, p).wait_recv()
        arrived = home[p].reshape(halves, LANES)
        a_low, a_high, b_low, b_high = [mm(pick, arrived) for pick in picks]
        left = a_low + pltpu.roll(a_high, HEAD_DIM, 1)
        right = b_high + pltpu.roll(b_low, HEAD_DIM, 1)
        att = jnp.where(lane_tok < HEAD_DIM, left, right)
        cols = slice(p * LANES, (p + 1) * LANES)
        att_out[:, cols] = att.astype(BF16)
        base = uncond[:, cols].astype(F32)
        guided = (base + GUIDE * (att - base)).astype(BF16)
        gsend[p] = guided.reshape(head_peers, peer_rows, LANES)
        loop(head_peers, lambda k: guide(p, k).start())
        keep = pltpu.make_async_copy(
            gsend.at[p, my_head], rows_hbm.at[my_head, p], store.at[1 + p]
        )
        keep.start()
        keeps.append(keep)

    att_store = pltpu.make_async_copy(att_out, att_hbm, store.at[0])
    att_store.start()
    for p in range(pairs):
        pair_wait(*backward, p).wait_send()
    for p in range(pairs):
        loop(head_peers, lambda k: guide_wait(p, k).wait_recv())
    for p in range(pairs):
        loop(head_peers, lambda k: guide_wait(p, k).wait_send())
    att_store.wait()
    for keep in keeps:
        keep.wait()


def finish_kernel(
    att_hbm,
    rows_hbm,
    zero_hbm,
    one_hbm,
    two_hbm,
    gain_hbm,
    bias_hbm,
    normed_hbm,
    att_out_hbm,
    first_hbm,
    second_hbm,
    third_hbm,
    att,
    zero,
    one,
    two,
    rows,
    gain,
    bias,
    first_out,
    second_out,
    third_out,
    normed,
    fetch,
    store,
):
    sources = (att_hbm, zero_hbm, one_hbm, two_hbm, rows_hbm, gain_hbm, bias_hbm)
    targets = (att, zero, one, two, rows, gain, bias)
    fetches = [
        pltpu.make_async_copy(src, dst, fetch.at[i])
        for i, (src, dst) in enumerate(zip(sources, targets))
    ]
    for one_fetch in fetches:
        one_fetch.start()
    stores = []

    def put(src, dst):
        copy = pltpu.make_async_copy(src, dst, store.at[len(stores)])
        copy.start()
        stores.append(copy)

    gap = 1.0 / STEP_GAP
    fetches[0].wait()
    put(att, att_out_hbm)
    fetches[1].wait()
    first = (att[...].astype(F32) - zero[...].astype(F32)) * gap
    first_out[...] = first.astype(BF16)
    put(first_out, first_hbm)
    fetches[2].wait()
    second = (first - one[...].astype(F32)) * gap
    second_out[...] = second.astype(BF16)
    put(second_out, second_hbm)
    fetches[3].wait()
    third = (second - two[...].astype(F32)) * gap
    third_out[...] = third.astype(BF16)
    put(third_out, third_hbm)
    for i in (4, 5, 6):
        fetches[i].wait()
    blocks = [rows[i, p] for i in range(rows.shape[0]) for p in range(rows.shape[1])]
    guided = jnp.concatenate(blocks, axis=1).astype(F32)
    inv = 1.0 / guided.shape[1]
    centered = guided - jnp.sum(guided, axis=1, keepdims=True) * inv
    var = jnp.sum(centered * centered, axis=1, keepdims=True) * inv
    scaled = centered * lax.rsqrt(var + EPS) * gain[...].reshape(1, -1)
    normed[...] = (scaled + bias[...].reshape(1, -1)).astype(BF16)
    put(normed, normed_hbm)
    for one_store in stores:
        one_store.wait()


def on_device(
    groups,
    head_peers,
    qkv,
    token_rank,
    cluster_sizes,
    cluster_owner,
    cache_zero,
    cache_one,
    cache_two,
    cache_uncond,
    norm_gain,
    norm_bias,
):
    heads, toks = token_rank.shape
    pairs = heads // 2
    width = norm_gain.shape[0]
    mine = cache_zero.shape[1]
    share = 2 * toks // groups
    slots = -(-share // 32) * 32
    half = slots // 2
    chunk = math.gcd(groups, max(256 // slots, 1))
    tag_lanes = -(-pairs * slots // LANES) * LANES
    peer_rows = toks // head_peers
    hbm = pl.BlockSpec(memory_space=pltpu.HBM)
    att, rows = pl.pallas_call(
        functools.partial(exchange_kernel, groups, head_peers),
        out_shape=(
            jax.ShapeDtypeStruct((toks, mine), BF16),
            jax.ShapeDtypeStruct((head_peers, pairs, peer_rows, LANES), BF16),
        ),
        in_specs=[hbm] * 5,
        out_specs=[hbm] * 2,
        scratch_shapes=[
            pltpu.VMEM(qkv.shape, BF16),
            pltpu.VMEM(token_rank.shape, jnp.int32),
            pltpu.VMEM(cluster_sizes.shape, jnp.int32),
            pltpu.VMEM(cluster_owner.shape, jnp.int32),
            pltpu.VMEM(cache_uncond.shape, BF16),
            pltpu.VMEM((toks, mine), BF16),
            pltpu.VMEM((pairs, groups, slots + half, LANES), BF16),
            pltpu.VMEM((pairs, groups, slots + half, LANES), BF16),
            pltpu.VMEM((1, groups, 1, tag_lanes), F32),
            pltpu.VMEM((1, groups, 1, tag_lanes), F32),
            pltpu.VMEM((pairs, groups, half, LANES), BF16),
            pltpu.VMEM((pairs, groups, half, LANES), BF16),
            pltpu.VMEM((pairs, head_peers, peer_rows, LANES), BF16),
            pltpu.VMEM((LANES, toks), F32),
            pltpu.VMEM((pairs * groups // chunk, chunk * slots, 1), F32),
            pltpu.SemaphoreType.DMA((5,)),
            pltpu.SemaphoreType.DMA((1 + pairs,)),
            pltpu.SemaphoreType.DMA((1,)),
            pltpu.SemaphoreType.DMA((1,)),
            pltpu.SemaphoreType.DMA((pairs,)),
            pltpu.SemaphoreType.DMA((pairs,)),
            pltpu.SemaphoreType.DMA((pairs,)),
            pltpu.SemaphoreType.DMA((pairs,)),
            pltpu.SemaphoreType.DMA((pairs, head_peers)),
            pltpu.SemaphoreType.DMA((pairs, head_peers)),
        ],
        compiler_params=pltpu.CompilerParams(
            collective_id=0, has_side_effects=True, vmem_limit_bytes=56 * 1024 * 1024
        ),
        name="exchange",
    )(qkv, token_rank, cluster_sizes, cluster_owner, cache_uncond)
    piece = jax.ShapeDtypeStruct((toks, mine), BF16)
    return pl.pallas_call(
        finish_kernel,
        out_shape=(jax.ShapeDtypeStruct((peer_rows, width), BF16), piece, piece, piece, piece),
        in_specs=[hbm] * 7,
        out_specs=[hbm] * 5,
        scratch_shapes=[
            *[pltpu.VMEM((toks, mine), BF16)] * 4,
            pltpu.VMEM((head_peers, pairs, peer_rows, LANES), BF16),
            pltpu.VMEM((width,), F32),
            pltpu.VMEM((width,), F32),
            *[pltpu.VMEM((toks, mine), BF16)] * 3,
            pltpu.VMEM((peer_rows, width), BF16),
            pltpu.SemaphoreType.DMA((7,)),
            pltpu.SemaphoreType.DMA((5,)),
        ],
        compiler_params=pltpu.CompilerParams(vmem_limit_bytes=56 * 1024 * 1024),
        name="finish",
    )(
        att,
        rows,
        cache_zero,
        cache_one,
        cache_two,
        norm_gain,
        norm_bias,
    )


def solution(mesh):
    sides = P("tok", "head")
    return jax.shard_map(
        functools.partial(on_device, mesh.shape["tok"], mesh.shape["head"]),
        mesh=mesh,
        in_specs=(
            P(None, "tok", "head"),
            P("head", "tok"),
            P("head", None),
            P("head", None),
            sides,
            sides,
            sides,
            sides,
            P(),
            P(),
        ),
        out_specs=(P(("tok", "head"), None), sides, sides, sides, sides),
        check_vma=False,
    )
```
